256 devices in a mesh: tok: 8 (over y, z_hi), hid: 32 (over z_lo, x, core).
Axes of the slice: x: 4, y: 4, z: 8 (z_hi: 2, z_lo: 4; z = z_hi * 4 + z_lo), core: 2. Of those that a mesh axis runs over, the one named last changes fastest.
Arguments:
- student_in: bfloat16 [1024, 8192], P('hid', 'tok'), may hold values from -6 to 6
- target_delta: bfloat16 [1024, 8192], P('hid', 'tok'), may hold values from -3 to 3
- gate_weight: bfloat16 [8192, 16384], P('tok', 'hid'), may hold values from -0.0625 to 0.0625
- up_weight: bfloat16 [8192, 16384], P('tok', 'hid'), may hold values from -0.0625 to 0.0625
- down_weight: bfloat16 [16384, 8192], P('hid', 'tok'), may hold values from -0.046875 to 0.046875
- block_mask: int32 [3, 64, 128], P(None, 'tok', 'hid'), may hold values from 0 to 1, as said below
Outputs:
- student_out: bfloat16 [1024, 8192], P('hid', 'tok')
- input_grad: bfloat16 [1024, 8192], P('hid', 'tok')
- gate_wgrad: float32 [8192, 16384], P('tok', 'hid')
- up_wgrad: float32 [8192, 16384], P('tok', 'hid')
- down_wgrad: float32 [16384, 8192], P('hid', 'tok')
The draws below stay inside these ranges and needn't reach their ends.
Inputs may be any that keep to these rules, and one draw needn't show every extreme that they name: `block_mask`: each entry is 0 or 1 (1 keeps a 128 x 128 block of weights); the share of ones differs from one block column of hidden units to another.
All inputs are finite; a program needn't handle non-finite values.
Results may differ from the reference program's by a relative error of at most 0.0056.
Values may be sent and summed in bfloat16 or wider, within the bound.
A program may use at most 64 MiB of HBM per device.

```python
import jax
import jax.numpy as jnp
from jax import lax

D = 8192
FF = 16384
BLOCK = 128
TOKENS = 1024


def draw_block_mask(key, part):
    level_key, coin_key = jax.random.split(jax.random.fold_in(key, 17))
    levels = jax.random.randint(level_key, (3, 1, FF // BLOCK), 1, 8)
    coins = jax.random.randint(coin_key, (3, D // BLOCK, FF // BLOCK), 0, 8)
    return (coins < levels).astype(jnp.int32)


def level_of(rng, dims, cuts, least, top_value):
    gain = 1.0
    for position, parts in cuts:
        draws = jax.random.uniform(jax.random.fold_in(jax.random.fold_in(rng, 6), position), (parts,), jnp.float32, least / len(cuts), top_value / len(cuts))
        gain = gain * jnp.repeat(jnp.exp(draws), dims[position] // parts).reshape((-1,) + (1,) * (len(dims) - 1 - position))
    return gain


def bell_draw(stream_key, shape, spread, bound, cuts=(), dtype=jnp.bfloat16):
    values = jax.random.normal(stream_key, shape, jnp.float32) * spread
    if len(cuts) > 0:
        values = level_of(stream_key, shape, cuts, -0.22, 0.18) * values
    return jnp.clip(values, min=-bound, max=bound).astype(dtype)


def setup_inputs(seed: int = 0) -> dict:
    key_of = jax.random.split(jax.random.key(seed), 7)
    return {
        "student_in": bell_draw(key_of[0], (TOKENS, D), 1.0, 6.0, ((0, 32), (1, 8))),
        "target_delta": bell_draw(key_of[1], (TOKENS, D), 0.5, 3.0, ((0, 32), (1, 8))),
        "gate_weight": bell_draw(key_of[2], (D, FF), D ** -0.5, 0.0625, ((0, 8), (1, 32))),
        "up_weight": bell_draw(key_of[3], (D, FF), D ** -0.5, 0.0625, ((0, 8), (1, 32))),
        "down_weight": bell_draw(key_of[4], (FF, D), FF ** -0.5, 0.046875, ((0, 32), (1, 8))),
        "block_mask": draw_block_mask(jax.random.fold_in(key_of[6], 71), 0),
    }


def widen(blocks):
    return jnp.repeat(jnp.repeat(blocks, BLOCK, axis=0), BLOCK, axis=1)

def reference(student_in, target_delta, gate_weight, up_weight, down_weight, block_mask):
    gate_mask = widen(block_mask[0]).astype(jnp.bfloat16)
    up_mask = widen(block_mask[1]).astype(jnp.bfloat16)
    down_mask = widen(block_mask[2]).T.astype(jnp.bfloat16)
    gate_eff = gate_weight * gate_mask
    up_eff = up_weight * up_mask
    down_eff = down_weight * down_mask
    gate = jnp.dot(student_in, gate_eff, preferred_element_type=jnp.float32)
    up = jnp.dot(student_in, up_eff, preferred_element_type=jnp.float32)
    sigma = jax.nn.sigmoid(gate)
    swish = gate * sigma
    hidden = (swish * up).astype(jnp.bfloat16)
    output_sum = jnp.dot(hidden, down_eff, preferred_element_type=jnp.float32)
    error = (output_sum - target_delta.astype(jnp.float32)).astype(jnp.bfloat16)
    by_cols = (((1,), (1,)), ((), ()))
    by_rows = (((0,), (0,)), ((), ()))
    hidden_grad = lax.dot_general(error, down_eff, by_cols, preferred_element_type=jnp.float32)
    gate_grad = (hidden_grad * up * (sigma + gate * sigma * (1.0 - sigma))).astype(jnp.bfloat16)
    up_grad = (hidden_grad * swish).astype(jnp.bfloat16)
    factor = 1.0 / jnp.sqrt(jnp.float32(TOKENS))
    gate_wgrad = lax.dot_general(student_in, gate_grad, by_rows, preferred_element_type=jnp.float32) * gate_mask.astype(jnp.float32) * factor
    up_wgrad = lax.dot_general(student_in, up_grad, by_rows, preferred_element_type=jnp.float32) * up_mask.astype(jnp.float32) * factor
    down_wgrad = lax.dot_general(hidden, error, by_rows, preferred_element_type=jnp.float32) * down_mask.astype(jnp.float32) * factor
    input_grad = lax.dot_general(gate_grad, gate_eff, by_cols, preferred_element_type=jnp.float32)
    input_grad = input_grad + lax.dot_general(up_grad, up_eff, by_cols, preferred_element_type=jnp.float32)
    return (output_sum.astype(jnp.bfloat16), input_grad.astype(jnp.bfloat16), gate_wgrad, up_wgrad, down_wgrad)
```

```python
import jax
import jax.numpy as jnp
from jax import lax
from jax.experimental import pallas as pl
from jax.experimental.pallas import tpu as pltpu
from jax.sharding import PartitionSpec as P

BF = jnp.bfloat16
F32 = jnp.float32
CHUNKS = 2
LAG = 5
T = 512
R = 16
CHIP = 2 * R
XB = 8 * R
Q = 64
D = 1024
H = 512
COPIES = 220

NN = (((1,), (0,)), ((), ()))
NT = (((1,), (1,)), ((), ()))
TN = (((0,), (0,)), ((), ()))


def mm(a, b, dims):
    return lax.dot_general(a, b, dims, preferred_element_type=F32)


def kernel(
    x_in, t_in, gw, uw, dw, bm,
    out, ig, gwg, uwg, dwg,
    weff, deff, xall, tch, tmp, ps2, own2, yl2, zs2, zl2, gu, hall,
    ss4, sl4, of4, xs4, xl4, zs4, zl4, osw, oland,
    eall, ps6, own6, yl6, zs6, zl6, gall,
    ss8, sl8, of8, xs8, xl8, zs8, zl8, isw, iland,
    wg, dg,
    send_sems, recv_sems, loc_sems,
):
    tok = lax.axis_index("tok")
    hid = lax.axis_index("hid")
    y, zh = lax.div(tok, 2), lax.rem(tok, 2)
    c, x, zl = lax.rem(hid, 2), lax.rem(lax.div(hid, 2), 4), lax.div(hid, 8)

    def dev(y=y, zh=zh, zl=zl, x=x, c=c):
        return {"tok": y * 2 + zh, "hid": (zl * 4 + x) * 2 + c}

    def plus(a, d):
        return lax.rem(a + d, 4)

    sib = dev(c=1 - c)
    xp = [dev(x=plus(x, d)) for d in (1, 2, 3)]
    zp = [dev(zl=plus(zl, d)) for d in (1, 2, 3)]
    yp = [dev(y=plus(y, d)) for d in (1, 2, 3)]
    far = dev(zh=1 - zh)
    peers = [sib, far] + xp + zp + yp

    def rows(start, size):
        return pl.ds(pl.multiple_of(start, 16), size)

    def half(which):
        return pl.ds(pl.multiple_of(which * H, H), H)

    mine, other = half(c), half(1 - c)
    copies = []

    def send(src, dst, device):
        i = len(copies)
        copy = pltpu.make_async_remote_copy(
            src_ref=src, dst_ref=dst, send_sem=send_sems.at[i], recv_sem=recv_sems.at[i],
            device_id=device, device_id_type=pl.DeviceIdType.MESH,
        )
        copy.start()
        copies.append(copy)
        return copy

    def arrived(group):
        for copy in group:
            copy.wait_recv()

    locals_ = []

    def local(src, dst):
        copy = pltpu.make_async_copy(src, dst, loc_sems.at[len(locals_)])
        copy.start()
        locals_.append(copy)
        return copy

    barrier = pltpu.get_barrier_semaphore()
    for peer in peers:
        pl.semaphore_signal(barrier, inc=1, device_id=peer, device_id_type=pl.DeviceIdType.MESH)
    pl.semaphore_wait(barrier, len(peers))

    block = x * XB + zl * CHIP
    first = []
    for k in range(CHUNKS):
        here = xall.at[k, rows(block + c * R, R), mine]
        there = xall.at[k, rows(block + c * R, R), other]
        first.append([send(x_in.at[pl.ds(k * R, R), other], there, sib),
                      local(x_in.at[pl.ds(k * R, R), mine], here)])
    targets = []
    for k in range(CHUNKS):
        spot = tch.at[k, rows(c * R, R)]
        targets.append([send(t_in.at[pl.ds(k * R, R), other], spot, sib),
                        local(t_in.at[pl.ds(k * R, R), mine], spot)])

    def mask_weights():
        @pl.loop(0, 8)
        def _(a):
            at = pl.ds(pl.multiple_of(a * 128, 128), 128)
            for b in range(4):
                lanes = pl.ds(b * 128, 128)
                weff[at, lanes] = (gw[at, lanes].astype(F32) * bm[0, a, b].astype(F32)).astype(BF)
                weff[at, pl.ds(H + b * 128, 128)] = (
                    uw[at, lanes].astype(F32) * bm[1, a, b].astype(F32)
                ).astype(BF)
                deff[lanes, at] = (dw[lanes, at].astype(F32) * bm[2, a, b].astype(F32)).astype(BF)

    def gather_hid(k, buf):
        own = buf.at[k, rows(block, CHIP), mine]
        zc = [send(own, own, p) for p in zp]
        yield
        arrived(zc)
        col = buf.at[k, rows(x * XB, XB), mine]
        xc = [send(col, col, p) for p in xp]
        sc = [send(col, col, sib)]
        for d, xcopy in enumerate(xc):
            yield
            arrived([xcopy])
            got = buf.at[k, rows(plus(x, 3 - d) * XB, XB), mine]
            sc.append(send(got, got, sib))
        yield
        arrived(sc)

    def scatter_tok(k, product, ps, own, yland, zs, zland, width):
        yc = []
        for part in range(2):
            zz = 1 - zh if part == 0 else zh

            @pl.loop(0, width // H)
            def _(n):
                lanes = pl.ds(pl.multiple_of(n * H, H), H)
                value = product(k, zz, lanes)
                tmp[:, lanes] = value
                ps[k, part, :, lanes] = value.astype(BF)

            own[k, part] = tmp[rows(y * Q, Q), pl.ds(0, width)]
            yc.append([send(ps.at[k, part, rows(plus(y, d) * Q, Q)], yland.at[k, part, 3 - d], yp[d - 1])
                       for d in (1, 2, 3)])
        yield
        arrived(yc[0])
        total = own[k, 0]
        for d in range(3):
            total = total + yland[k, 0, d].astype(F32)
        zs[k] = total.astype(zs.dtype)
        zc = send(zs.at[k], zland.at[k], far)
        yield
        arrived(yc[1])
        total = own[k, 1]
        for d in range(3):
            total = total + yland[k, 1, d].astype(F32)
        own[k, 1] = total
        yield
        arrived([zc])

    def gather_tok(k, buf):
        own = buf.at[k, rows(zh * 4 * Q + y * Q, Q)]
        zc = send(own, own, far)
        yc = [send(own, own, p) for p in yp]
        yield
        arrived([zc])
        got = buf.at[k, rows((1 - zh) * 4 * Q + y * Q, Q)]
        yc += [send(got, got, p) for p in yp]
        yield
        arrived(yc)

    def scatter_hid(k, product, ss, sl, of, xs, xl, zs, zland):
        ss[k] = product(k, other).astype(ss.dtype)
        sc = send(ss.at[k], sl.at[k], sib)
        of[k] = product(k, mine)
        yield
        arrived([sc])
        xc = []
        for d in (2, 1, 3):
            at = rows(plus(x, d) * XB, XB)
            xs[k, d - 1] = (of[k, at] + sl[k, at].astype(F32)).astype(BF)
            xc.append(send(xs.at[k, d - 1], xl.at[k, 3 - d], xp[d - 1]))
        at = rows(x * XB, XB)
        of[k, at] = of[k, at] + sl[k, at].astype(F32)
        yield
        arrived(xc)
        total = of[k, at]
        for d in range(3):
            total = total + xl[k, d].astype(F32)
        of[k, at] = total
        zc = []
        for d in (1, 2, 3):
            zs[k, d - 1] = of[k, rows(x * XB + plus(zl, d) * CHIP, CHIP)].astype(BF)
            zc.append(send(zs.at[k, d - 1], zland.at[k, 3 - d], zp[d - 1]))
        yield
        arrived(zc)

    def scattered(k, of, zland):
        total = of[k, rows(block, CHIP)]
        for d in range(3):
            total = total + zland[k, d].astype(F32)
        return total

    def chain(k):
        arrived(first[k][:1])
        first[k][1].wait()
        yield from gather_hid(k, xall)

        def inputs_by_weights(k, zz, lanes):
            return mm(xall[k, rows(zz * 4 * Q, 4 * Q), :], weff[:, lanes], NN)

        yield from scatter_tok(k, inputs_by_weights, ps2, own2, yl2, zs2, zl2, 2 * H)
        gu[k] = own2[k, 1] + zl2[k].astype(F32)
        gate, up = gu[k, :, :H], gu[k, :, H:]
        hall[k, rows(zh * 4 * Q + y * Q, Q), :] = (gate * jax.nn.sigmoid(gate) * up).astype(BF)
        yield from gather_tok(k, hall)

        def hidden_by_down(k, lanes):
            return mm(hall[k], deff[:, lanes], NN)

        yield from scatter_hid(k, hidden_by_down, ss4, sl4, of4, xs4, xl4, zs4, zl4)
        total = scattered(k, of4, zl4)
        arrived(targets[k][:1])
        targets[k][1].wait()
        eall[k, rows(block, CHIP), mine] = (total - tch[k].astype(F32)).astype(BF)
        osw[k] = total.astype(BF)
        out_swap[k] = send(osw.at[k, rows((1 - c) * R, R)], oland.at[k], sib)
        yield from gather_hid(k, eall)

        def error_by_down(k, zz, lanes):
            return mm(eall[k, rows(zz * 4 * Q, 4 * Q), :], deff[...], NT)

        yield from scatter_tok(k, error_by_down, ps6, own6, yl6, zs6, zl6, H)
        hidden_grad = own6[k, 1] + zl6[k].astype(F32)
        gate, up = gu[k, :, :H], gu[k, :, H:]
        sigma = jax.nn.sigmoid(gate)
        at = rows(zh * 4 * Q + y * Q, Q)
        gall[k, at, :H] = (hidden_grad * up * (sigma + gate * sigma * (1.0 - sigma))).astype(BF)
        gall[k, at, H:] = (hidden_grad * (gate * sigma)).astype(BF)
        yield from gather_tok(k, gall)

        def grads_by_weights(k, which):
            return mm(gall[k], weff[which, :], NT)

        yield from scatter_hid(k, grads_by_weights, ss8, sl8, of8, xs8, xl8, zs8, zl8)
        isw[k] = scattered(k, of8, zl8).astype(BF)
        in_swap[k] = send(isw.at[k, rows((1 - c) * R, R)], iland.at[k], sib)

    def scale(which, a, b):
        return bm[which, a, b].astype(F32) * (1.0 / 32.0)

    def weight_grads():
        @pl.loop(0, 2)
        def _(p):
            at = pl.ds(pl.multiple_of(p * 256, 256), 256)
            value = mm(hall[0, :, at], eall[0], TN) + mm(hall[1, :, at], eall[1], TN)
            for i in range(2):
                for a in range(8):
                    dg[pl.ds(pl.multiple_of(p * 256 + i * 128, 128), 128), pl.ds(a * 128, 128)] = (
                        value[i * 128 : i * 128 + 128, a * 128 : a * 128 + 128] * scale(2, a, p * 2 + i)
                    )

        local(dg, dwg)

        @pl.loop(0, 4)
        def _(p):
            at = pl.ds(pl.multiple_of(p * 256, 256), 256)
            value = mm(xall[0, :, at], gall[0], TN) + mm(xall[1, :, at], gall[1], TN)
            for i in range(2):
                for b in range(8):
                    wg[pl.ds(pl.multiple_of(p * 256 + i * 128, 128), 128), pl.ds(b * 128, 128)] = (
                        value[i * 128 : i * 128 + 128, b * 128 : b * 128 + 128]
                        * scale(b // 4, p * 2 + i, b % 4)
                    )

        local(wg.at[:, pl.ds(0, H)], gwg)
        local(wg.at[:, pl.ds(H, H)], uwg)

    out_swap, in_swap = {}, {}
    chains = [chain(k) for k in range(CHUNKS)]
    done = [False] * CHUNKS
    masked = False
    step = 0
    wgrads_at = 10**6
    while not all(done):
        for k in range(CHUNKS):
            if step >= k * LAG and not done[k]:
                done[k] = next(chains[k], True) is True
        if not masked:
            mask_weights()
            masked = True
        step += 1
    weight_grads()
    for k in range(CHUNKS):
        at = pl.ds(k * R, R)
        arrived([out_swap[k], in_swap[k]])
        out[at, mine] = osw[k, rows(c * R, R)]
        out[at, other] = oland[k]
        ig[at, mine] = isw[k, rows(c * R, R)]
        ig[at, other] = iland[k]
    for copy in copies:
        copy.wait_send()
    for copy in locals_[2 * CHUNKS :]:
        copy.wait()


def per_device(student_in, target_delta, gate_weight, up_weight, down_weight, block_mask):
    C = CHUNKS
    vm = pltpu.VMEM

    def scatter_hid_scratch():
        return [
            vm((C, T, H), F32), vm((C, T, H), F32), vm((C, T, H), F32), vm((C, 3, XB, H), BF), vm((C, 3, XB, H), BF),
            vm((C, 3, CHIP, H), BF), vm((C, 3, CHIP, H), BF), vm((C, CHIP, H), BF), vm((C, R, H), BF),
        ]

    def scatter_tok_scratch(width, far_type):
        return [
            vm((C, 2, 4 * Q, width), BF), vm((C, 2, Q, width), F32), vm((C, 2, 3, Q, width), BF),
            vm((C, Q, width), far_type), vm((C, Q, width), far_type),
        ]

    vspec = pl.BlockSpec(memory_space=pltpu.VMEM)
    anys = pl.BlockSpec(memory_space=pl.ANY)
    return pl.pallas_call(
        kernel,
        out_shape=(
            jax.ShapeDtypeStruct((32, D), BF),
            jax.ShapeDtypeStruct((32, D), BF),
            jax.ShapeDtypeStruct((D, H), F32),
            jax.ShapeDtypeStruct((D, H), F32),
            jax.ShapeDtypeStruct((H, D), F32),
        ),
        in_specs=[vspec] * 5 + [pl.BlockSpec(memory_space=pltpu.SMEM)],
        out_specs=(vspec, vspec, anys, anys, anys),
        scratch_shapes=[
            vm((D, 2 * H), BF), vm((H, D), BF), vm((C, T, D), BF), vm((C, CHIP, H), BF), vm((4 * Q, 2 * H), F32),
            *scatter_tok_scratch(2 * H, F32), vm((C, Q, 2 * H), F32), vm((C, T, H), BF),
            *scatter_hid_scratch(),
            vm((C, T, D), BF), *scatter_tok_scratch(H, BF), vm((C, T, 2 * H), BF),
            *scatter_hid_scratch(),
            vm((D, 2 * H), F32), vm((H, D), F32),
            pltpu.SemaphoreType.DMA((COPIES,)), pltpu.SemaphoreType.DMA((COPIES,)), pltpu.SemaphoreType.DMA((8,)),
        ],
        compiler_params=pltpu.CompilerParams(
            collective_id=0, has_side_effects=True, vmem_limit_bytes=56 << 20
        ),
        cost_estimate=pl.CostEstimate(flops=9663676416, bytes_accessed=10 << 20, transcendentals=262144),
    )(student_in, target_delta, gate_weight, up_weight, down_weight, block_mask)


def solution(mesh):
    placed = (
        P("hid", "tok"),
        P("hid", "tok"),
        P("tok", "hid"),
        P("tok", "hid"),
        P("hid", "tok"),
        P(None, "tok", "hid"),
    )
    return jax.shard_map(
        per_device,
        mesh=mesh,
        in_specs=placed,
        out_specs=(
            P("hid", "tok"),
            P("hid", "tok"),
            P("tok", "hid"),
            P("tok", "hid"),
            P("hid", "tok"),
        ),
        check_vma=False,
    )
```

```python
import jax
import jax.numpy as jnp
from jax import lax
from jax.experimental import pallas as pl
from jax.experimental.pallas import tpu as pltpu
from jax.sharding import PartitionSpec as P

BF = jnp.bfloat16
F32 = jnp.float32
CHUNKS = 4
T = 256
CHIP = 16
XB = 4 * CHIP
Q = 32
D = 1024
H = 512
COPIES = 256
STEPS = 23
LAG = 1

NN = (((1,), (0,)), ((), ()))
NT = (((1,), (1,)), ((), ()))
TN = (((0,), (0,)), ((), ()))


def mm(a, b, dims):
    return lax.dot_general(a, b, dims, preferred_element_type=F32)


def kernel(
    x_in, t_in, gw, uw, dw, bm,
    out, ig, x_out, h_out, e_out, g_out,
    weff, deff, xall, tch, tmp, ps2, own2, yl2, zs2, zl2, gu, hall,
    ss4, sl4, of4, xs4, xl4, zs4, zl4, osw, oland,
    eall, ps6, own6, yl6, zs6, zl6, gall,
    ss8, sl8, of8, xs8, xl8, zs8, zl8, isw, iland,
    send_sems, recv_sems, loc_sems,
):
    tok = lax.axis_index("tok")
    hid = lax.axis_index("hid")
    y, zh = lax.div(tok, 2), lax.rem(tok, 2)
    c, x, zl = lax.rem(hid, 2), lax.rem(lax.div(hid, 2), 4), lax.div(hid, 8)

    def dev(y=y, zh=zh, zl=zl, x=x, c=c):
        return {"tok": y * 2 + zh, "hid": (zl * 4 + x) * 2 + c}

    def plus(a, d):
        return lax.rem(a + d, 4)

    sib = dev(c=1 - c)
    xp = [dev(x=plus(x, d)) for d in (1, 2, 3)]
    zp = [dev(zl=plus(zl, d)) for d in (1, 2, 3)]
    yp = [dev(y=plus(y, d)) for d in (1, 2, 3)]
    far = dev(zh=1 - zh)
    peers = [sib, far] + xp + zp + yp

    def rows(start, size):
        return pl.ds(pl.multiple_of(start, 16), size)

    def half(which):
        return pl.ds(pl.multiple_of(which * H, H), H)

    mine, other = half(c), half(1 - c)
    copies = []

    def send(src, dst, device):
        i = len(copies)
        copy = pltpu.make_async_remote_copy(
            src_ref=src, dst_ref=dst, send_sem=send_sems.at[i], recv_sem=recv_sems.at[i],
            device_id=device, device_id_type=pl.DeviceIdType.MESH,
        )
        copy.start()
        copies.append(copy)
        return copy

    def arrived(group):
        for copy in group:
            copy.wait_recv()

    locals_ = []

    def local(src, dst):
        copy = pltpu.make_async_copy(src, dst, loc_sems.at[len(locals_)])
        copy.start()
        locals_.append(copy)
        return copy

    barrier = pltpu.get_barrier_semaphore()
    for peer in peers:
        pl.semaphore_signal(barrier, inc=1, device_id=peer, device_id_type=pl.DeviceIdType.MESH)
    pl.semaphore_wait(barrier, len(peers))

    block = x * XB + zl * CHIP
    first = []
    for whole, buf, at in ((x_in, xall, block), (t_in, tch, 0)):
        for j in range(2):
            src = whole.at[pl.ds(j * CHIP, CHIP)]
            dst = buf.at[2 * c + j, rows(at, CHIP)]
            if whole is x_in:
                first.append([send(src.at[:, other], dst.at[:, other], sib), local(src.at[:, mine], dst.at[:, mine])])
            else:
                first.append([send(src.at[:, other], dst, sib), local(src.at[:, mine], dst)])

    def mask_weights():
        @pl.loop(0, 8)
        def _(a):
            at = pl.ds(pl.multiple_of(a * 128, 128), 128)
            for b in range(4):
                lanes = pl.ds(b * 128, 128)
                weff[at, lanes] = (gw[at, lanes].astype(F32) * bm[0, a, b].astype(F32)).astype(BF)
                weff[at, pl.ds(H + b * 128, 128)] = (
                    uw[at, lanes].astype(F32) * bm[1, a, b].astype(F32)
                ).astype(BF)
                deff[lanes, at] = (dw[lanes, at].astype(F32) * bm[2, a, b].astype(F32)).astype(BF)

    def gather_hid(k, buf):
        own = buf.at[k, rows(block, CHIP), mine]
        zc = [send(own, own, p) for p in zp]
        yield
        arrived(zc)
        col = buf.at[k, rows(x * XB, XB), mine]
        xc = [send(col, col, p) for p in xp]
        sc = [send(col, col, sib)]
        yield
        for d, xcopy in enumerate(xc):
            arrived([xcopy])
            got = buf.at[k, rows(plus(x, 3 - d) * XB, XB), mine]
            sc.append(send(got, got, sib))
        yield
        arrived(sc)

    def scatter_tok(k, product, ps, own, yland, zs, zland, width):
        @pl.loop(0, width // H)
        def _(n):
            lanes = pl.ds(pl.multiple_of(n * H, H), H)
            value = product(k, lanes)
            tmp[:, lanes] = value
            ps[k, :, lanes] = value.astype(BF)

        yc = []
        for part in range(2):
            base = (1 - zh if part == 0 else zh) * 4 * Q
            own[k, part] = tmp[rows(base + y * Q, Q), pl.ds(0, width)]
            yc.append([send(ps.at[k, rows(base + plus(y, d) * Q, Q)], yland.at[k, part, 3 - d], yp[d - 1])
                       for d in (2, 1, 3)])
        yield
        arrived(yc[0])
        total = own[k, 0]
        for d in range(3):
            total = total + yland[k, 0, d].astype(F32)
        zs[k] = total.astype(zs.dtype)
        zc = send(zs.at[k], zland.at[k], far)
        yield
        arrived(yc[1])
        total = own[k, 1]
        for d in range(3):
            total = total + yland[k, 1, d].astype(F32)
        own[k, 1] = total
        yield
        arrived([zc])

    def gather_tok(k, buf):
        own = buf.at[k, rows(zh * 4 * Q + y * Q, Q)]
        zc = send(own, own, far)
        yc = [send(own, own, p) for p in yp]
        yield
        arrived([zc])
        got = buf.at[k, rows((1 - zh) * 4 * Q + y * Q, Q)]
        yc += [send(got, got, p) for p in yp]
        yield
        arrived(yc)

    def scatter_hid(k, product, ss, sl, of, xs, xl, zs, zland):
        ss[k] = product(k, other).astype(ss.dtype)
        sc = send(ss.at[k], sl.at[k], sib)
        of[k] = product(k, mine)
        yield
        arrived([sc])
        xc = []
        for d in (2, 1, 3):
            at = rows(plus(x, d) * XB, XB)
            xs[k, d - 1] = (of[k, at] + sl[k, at].astype(F32)).astype(BF)
            xc.append(send(xs.at[k, d - 1], xl.at[k, 3 - d], xp[d - 1]))
        at = rows(x * XB, XB)
        of[k, at] = of[k, at] + sl[k, at].astype(F32)
        yield
        arrived(xc)
        total = of[k, at]
        for d in range(3):
            total = total + xl[k, d].astype(F32)
        of[k, at] = total
        zc = []
        for d in (1, 2, 3):
            zs[k, d - 1] = of[k, rows(x * XB + plus(zl, d) * CHIP, CHIP)].astype(BF)
            zc.append(send(zs.at[k, d - 1], zland.at[k, 3 - d], zp[d - 1]))
        yield
        arrived(zc)

    def scattered(k, of, zland):
        total = of[k, rows(block, CHIP)]
        for d in range(3):
            total = total + zland[k, d].astype(F32)
        return total

    def chain(k):
        panel = rows(zh * 4 * Q + y * Q, Q)
        tokens = pl.ds(k * T, T)
        yield from gather_hid(k, xall)
        local(xall.at[k], x_out.at[tokens])

        def inputs_by_weights(k, lanes):
            return mm(xall[k], weff[:, lanes], NN)

        yield from scatter_tok(k, inputs_by_weights, ps2, own2, yl2, zs2, zl2, 2 * H)
        gu[k] = own2[k, 1] + zl2[k].astype(F32)
        gate, up = gu[k, :, :H], gu[k, :, H:]
        hall[k, panel, :] = (gate * jax.nn.sigmoid(gate) * up).astype(BF)
        yield from gather_tok(k, hall)
        local(hall.at[k], h_out.at[tokens])

        def hidden_by_down(k, lanes):
            return mm(hall[k], deff[:, lanes], NN)

        yield from scatter_hid(k, hidden_by_down, ss4, sl4, of4, xs4, xl4, zs4, zl4)
        total = scattered(k, of4, zl4)
        eall[k, rows(block, CHIP), mine] = (total - tch[k].astype(F32)).astype(BF)
        osw[k] = total.astype(BF)
        yield from gather_hid(k, eall)
        local(eall.at[k], e_out.at[tokens])

        def error_by_down(k, lanes):
            return mm(eall[k], deff[...], NT)

        yield from scatter_tok(k, error_by_down, ps6, own6, yl6, zs6, zl6, H)
        hidden_grad = own6[k, 1] + zl6[k].astype(F32)
        gate, up = gu[k, :, :H], gu[k, :, H:]
        sigma = jax.nn.sigmoid(gate)
        gall[k, panel, :H] = (hidden_grad * up * (sigma + gate * sigma * (1.0 - sigma))).astype(BF)
        gall[k, panel, H:] = (hidden_grad * (gate * sigma)).astype(BF)
        yield from gather_tok(k, gall)
        local(gall.at[k], g_out.at[tokens])

        def grads_by_weights(k, which):
            return mm(gall[k], weff[which, :], NT)

        yield from scatter_hid(k, grads_by_weights, ss8, sl8, of8, xs8, xl8, zs8, zl8)
        isw[k] = scattered(k, of8, zl8).astype(BF)

    for remote, near in first:
        arrived([remote])
        near.wait()
    chains = [chain(k) for k in range(CHUNKS)]
    for step in range(STEPS + LAG * (CHUNKS - 1)):
        for k in range(CHUNKS):
            if 0 <= step - k * LAG < STEPS:
                next(chains[k], None)
        if step == 0:
            mask_weights()
    swaps = [[send(held.at[2 * (1 - c) + j], land.at[j], sib) for j in range(2)]
             for held, land in ((osw, oland), (isw, iland))]
    for j in range(2):
        at = pl.ds(j * CHIP, CHIP)
        for swap, held, land, result in zip(swaps, (osw, isw), (oland, iland), (out, ig)):
            result[at, mine] = held[2 * c + j]
            arrived([swap[j]])
            result[at, other] = land[j]
    for copy in copies:
        copy.wait_send()
    for copy in locals_[4:]:
        copy.wait()


def weight_grads(bm, x, h, e, g, out_in, ig_in, out, ig, gwg, uwg, dwg):
    p = pl.program_id(0)
    out[...] = out_in[...]
    ig[...] = ig_in[...]
    value = mm(x[...], g[...], TN)
    for i in range(2):
        for b in range(8):
            to = (gwg, uwg)[b // 4]
            to[pl.ds(i * 128, 128), pl.ds(b % 4 * 128, 128)] = (
                value[i * 128 : i * 128 + 128, b * 128 : b * 128 + 128]
                * (bm[b // 4, p * 2 + i, b % 4].astype(F32) * (1.0 / 32.0))
            )
    value = mm(h[...], e[...], TN)
    for a in range(8):
        dwg[:, pl.ds(a * 128, 128)] = value[:, a * 128 : a * 128 + 128] * (
            bm[2, a, p].astype(F32) * (1.0 / 32.0)
        )


def per_device(student_in, target_delta, gate_weight, up_weight, down_weight, block_mask):
    C = CHUNKS
    vm = pltpu.VMEM

    def scatter_hid_scratch():
        return [
            vm((C, T, H), F32), vm((C, T, H), F32), vm((C, T, H), F32), vm((C, 3, XB, H), BF), vm((C, 3, XB, H), BF),
            vm((C, 3, CHIP, H), BF), vm((C, 3, CHIP, H), BF), vm((C, CHIP, H), BF), vm((2, CHIP, H), BF),
        ]

    def scatter_tok_scratch(width, far_type):
        return [
            vm((C, T, width), BF), vm((C, 2, Q, width), F32), vm((C, 2, 3, Q, width), BF),
            vm((C, Q, width), far_type), vm((C, Q, width), far_type),
        ]

    vspec = pl.BlockSpec(memory_space=pltpu.VMEM)
    anys = pl.BlockSpec(memory_space=pl.ANY)
    small, square = jax.ShapeDtypeStruct((2 * CHIP, D), BF), jax.ShapeDtypeStruct((C * T, D), BF)
    out, ig, x, h, e, g = pl.pallas_call(
        kernel,
        out_shape=(small, small, square, jax.ShapeDtypeStruct((C * T, H), BF), square, square),
        in_specs=[vspec] * 5 + [pl.BlockSpec(memory_space=pltpu.SMEM)],
        out_specs=(vspec, vspec, anys, anys, anys, anys),
        scratch_shapes=[
            vm((D, 2 * H), BF), vm((H, D), BF), vm((C, T, D), BF), vm((C, CHIP, H), BF), vm((T, 2 * H), F32),
            *scatter_tok_scratch(2 * H, F32), vm((C, Q, 2 * H), F32), vm((C, T, H), BF),
            *scatter_hid_scratch(),
            vm((C, T, D), BF), *scatter_tok_scratch(H, BF), vm((C, T, 2 * H), BF),
            *scatter_hid_scratch(),
            pltpu.SemaphoreType.DMA((COPIES,)), pltpu.SemaphoreType.DMA((COPIES,)), pltpu.SemaphoreType.DMA((20,)),
        ],
        compiler_params=pltpu.CompilerParams(
            collective_id=0, has_side_effects=True, vmem_limit_bytes=56 << 20
        ),
        cost_estimate=pl.CostEstimate(flops=6442450944, bytes_accessed=10 << 20, transcendentals=262144),
    )(student_in, target_delta, gate_weight, up_weight, down_weight, block_mask)
    full = lambda *shape: pl.BlockSpec(shape, lambda p: (0, 0))
    return pl.pallas_call(
        weight_grads,
        grid=(4,),
        out_shape=(
            small,
            small,
            jax.ShapeDtypeStruct((D, H), F32),
            jax.ShapeDtypeStruct((D, H), F32),
            jax.ShapeDtypeStruct((H, D), F32),
        ),
        in_specs=[
            pl.BlockSpec(memory_space=pltpu.SMEM),
            pl.BlockSpec((C * T, 256), lambda p: (0, p)),
            pl.BlockSpec((C * T, 128), lambda p: (0, p)),
            full(C * T, D),
            full(C * T, D),
            full(2 * CHIP, D),
            full(2 * CHIP, D),
        ],
        out_specs=(
            full(2 * CHIP, D),
            full(2 * CHIP, D),
            pl.BlockSpec((256, H), lambda p: (p, 0)),
            pl.BlockSpec((256, H), lambda p: (p, 0)),
            pl.BlockSpec((128, D), lambda p: (p, 0)),
        ),
        compiler_params=pltpu.CompilerParams(vmem_limit_bytes=40 << 20),
        cost_estimate=pl.CostEstimate(flops=3221225472, bytes_accessed=13 << 20, transcendentals=0),
    )(block_mask, x, h, e, g, out, ig)


def solution(mesh):
    placed = (
        P("hid", "tok"),
        P("hid", "tok"),
        P("tok", "hid"),
        P("tok", "hid"),
        P("hid", "tok"),
        P(None, "tok", "hid"),
    )
    return jax.shard_map(
        per_device,
        mesh=mesh,
        in_specs=placed,
        out_specs=(
            P("hid", "tok"),
            P("hid", "tok"),
            P("tok", "hid"),
            P("tok", "hid"),
            P("hid", "tok"),
        ),
        check_vma=False,
    )
```

```python
import jax
import jax.numpy as jnp
from jax import lax
from jax.experimental import pallas as pl
from jax.experimental.pallas import tpu as pltpu
from jax.sharding import PartitionSpec as P

BF = jnp.bfloat16
F32 = jnp.float32
CHUNKS = 4
T = 256
CHIP = 16
XB = 4 * CHIP
Q = 32
D = 1024
H = 512
COPIES = 112
STEPS = 23
LAG = 1

NN = (((1,), (0,)), ((), ()))
NT = (((1,), (1,)), ((), ()))
TN = (((0,), (0,)), ((), ()))


def mm(a, b, dims):
    return lax.dot_general(a, b, dims, preferred_element_type=F32)


def kernel(
    x_in, t_in, gw_in, uw_in, dw_in, bm_in,
    out, ig, x_out, h_out, e_out, g_out,
    weff, deff, xall, tch, tmp, ps2, own2, yl2, zs2, zl2, gu, hall,
    ss4, sl4, of4, xs4, xl4, zs4, zl4, osw, oland,
    eall, ps6, own6, yl6, zs6, zl6, gall,
    ss8, sl8, of8, xs8, xl8, zs8, zl8, isw, iland,
    gw, uw, dw, bm,
    send_sems, recv_sems, loc_sems,
):
    tok = lax.axis_index("tok")
    hid = lax.axis_index("hid")
    y, zh = lax.div(tok, 2), lax.rem(tok, 2)
    c, x, zl = lax.rem(hid, 2), lax.rem(lax.div(hid, 2), 4), lax.div(hid, 8)

    def dev(y=y, zh=zh, zl=zl, x=x, c=c):
        return {"tok": y * 2 + zh, "hid": (zl * 4 + x) * 2 + c}

    def plus(a, d):
        return lax.rem(a + d, 4)

    sib = dev(c=1 - c)
    xp = [dev(x=plus(x, d)) for d in (1, 2, 3)]
    zp = [dev(zl=plus(zl, d)) for d in (1, 2, 3)]
    yp = [dev(y=plus(y, d)) for d in (1, 2, 3)]
    far = dev(zh=1 - zh)
    peers = [sib, far] + xp + zp + yp

    def rows(start, size):
        return pl.ds(pl.multiple_of(start, 16), size)

    def half(which):
        return pl.ds(pl.multiple_of(which * H, H), H)

    mine, other = half(c), half(1 - c)
    groups = []

    def send(pairs, whole):
        i = len(groups)
        for src, dst, device in pairs:
            pltpu.make_async_remote_copy(
                src_ref=src, dst_ref=dst, send_sem=send_sems.at[i], recv_sem=recv_sems.at[i],
                device_id=device, device_id_type=pl.DeviceIdType.MESH,
            ).start()
        groups.append(
            pltpu.make_async_remote_copy(
                src_ref=whole, dst_ref=whole, send_sem=send_sems.at[i], recv_sem=recv_sems.at[i],
                device_id=sib, device_id_type=pl.DeviceIdType.MESH,
            )
        )
        return groups[-1]

    locals_ = []

    def local(src, dst):
        copy = pltpu.make_async_copy(src, dst, loc_sems.at[len(locals_)])
        copy.start()
        locals_.append(copy)
        return copy

    barrier = pltpu.get_barrier_semaphore()
    for peer in peers:
        pl.semaphore_signal(barrier, inc=1, device_id=peer, device_id_type=pl.DeviceIdType.MESH)
    for whole, held in ((bm_in, bm), (gw_in, gw), (uw_in, uw), (dw_in, dw)):
        local(whole, held)
    pl.semaphore_wait(barrier, len(peers))

    block = x * XB + zl * CHIP
    first = []
    for whole, buf, at in ((x_in, xall, block), (t_in, tch, 0)):
        for j in range(2):
            src = whole.at[pl.ds(j * CHIP, CHIP)]
            dst = buf.at[2 * c + j, rows(at, CHIP)]
            if whole is x_in:
                first.append(send([(src.at[:, other], dst.at[:, other], sib)], dst.at[:, other]))
                local(src.at[:, mine], dst.at[:, mine])
            else:
                first.append(send([(src.at[:, other], dst, sib)], dst))
                local(src.at[:, mine], dst)

    def mask_weights():
        for copy in locals_[:4]:
            copy.wait()

        @pl.loop(0, 8)
        def _(a):
            at = pl.ds(pl.multiple_of(a * 128, 128), 128)
            for b in range(4):
                lanes = pl.ds(b * 128, 128)
                weff[at, lanes] = (gw[at, lanes].astype(F32) * bm[0, b, a].astype(F32)).astype(BF)
                weff[at, pl.ds(H + b * 128, 128)] = (
                    uw[at, lanes].astype(F32) * bm[1, b, a].astype(F32)
                ).astype(BF)
                deff[lanes, at] = (dw[lanes, at].astype(F32) * bm[2, b, a].astype(F32)).astype(BF)

    def gather_hid(k, buf):
        own = buf.at[k, rows(block, CHIP), mine]
        zc = send([(own, own, p) for p in zp], buf.at[k, pl.ds(0, 3 * CHIP), mine])
        yield
        zc.wait_recv()
        col = buf.at[k, rows(x * XB, XB), mine]
        xc = send([(col, col, xp[d - 1]) for d in (2, 1, 3)], buf.at[k, pl.ds(0, 3 * XB), mine])
        s1 = send([(col, col, sib)], col)
        yield
        xc.wait_recv()
        got = [buf.at[k, rows(plus(x, d) * XB, XB), mine] for d in (1, 2, 3)]
        s2 = send([(g, g, sib) for g in got], buf.at[k, pl.ds(0, 3 * XB), mine])
        yield
        s1.wait_recv()
        s2.wait_recv()

    def scatter_tok(k, product, ps, own, yland, zs, zland, width):
        @pl.loop(0, width // H)
        def _(n):
            lanes = pl.ds(pl.multiple_of(n * H, H), H)
            value = product(k, lanes)
            tmp[:, lanes] = value
            ps[k, :, lanes] = value.astype(BF)

        yc = []
        for part in range(2):
            base = (1 - zh if part == 0 else zh) * 4 * Q
            own[k, part] = tmp[rows(base + y * Q, Q), pl.ds(0, width)]
            yc.append(send([(ps.at[k, rows(base + plus(y, d) * Q, Q)], yland.at[k, part, 3 - d], yp[d - 1])
                            for d in (2, 1, 3)], yland.at[k, part]))
        yield
        yc[0].wait_recv()
        total = own[k, 0]
        for d in range(3):
            total = total + yland[k, 0, d].astype(F32)
        zs[k] = total.astype(zs.dtype)
        zc = send([(zs.at[k], zland.at[k], far)], zland.at[k])
        yield
        yc[1].wait_recv()
        total = own[k, 1]
        for d in range(3):
            total = total + yland[k, 1, d].astype(F32)
        own[k, 1] = total
        yield
        zc.wait_recv()

    def gather_tok(k, buf):
        own = buf.at[k, rows(zh * 4 * Q + y * Q, Q)]
        three = buf.at[k, pl.ds(0, 3 * Q)]
        zc = send([(own, own, far)], own)
        y1 = send([(own, own, yp[d - 1]) for d in (2, 1, 3)], three)
        yield
        zc.wait_recv()
        got = buf.at[k, rows((1 - zh) * 4 * Q + y * Q, Q)]
        y2 = send([(got, got, yp[d - 1]) for d in (2, 1, 3)], three)
        yield
        y1.wait_recv()
        y2.wait_recv()

    def scatter_hid(k, product, ss, sl, of, xs, xl, zs, zland):
        ss[k] = product(k, other).astype(ss.dtype)
        sc = send([(ss.at[k], sl.at[k], sib)], sl.at[k])
        of[k] = product(k, mine)
        yield
        sc.wait_recv()
        pairs = []
        for d in (2, 1, 3):
            at = rows(plus(x, d) * XB, XB)
            xs[k, d - 1] = (of[k, at] + sl[k, at].astype(F32)).astype(BF)
            pairs.append((xs.at[k, d - 1], xl.at[k, 3 - d], xp[d - 1]))
        xc = send(pairs, xl.at[k])
        at = rows(x * XB, XB)
        of[k, at] = of[k, at] + sl[k, at].astype(F32)
        yield
        xc.wait_recv()
        total = of[k, at]
        for d in range(3):
            total = total + xl[k, d].astype(F32)
        of[k, at] = total
        pairs = []
        for d in (1, 2, 3):
            zs[k, d - 1] = of[k, rows(x * XB + plus(zl, d) * CHIP, CHIP)].astype(BF)
            pairs.append((zs.at[k, d - 1], zland.at[k, 3 - d], zp[d - 1]))
        zc = send(pairs, zland.at[k])
        yield
        zc.wait_recv()

    def scattered(k, of, zland):
        total = of[k, rows(block, CHIP)]
        for d in range(3):
            total = total + zland[k, d].astype(F32)
        return total

    def chain(k):
        panel = rows(zh * 4 * Q + y * Q, Q)
        tokens = pl.ds(k * T, T)
        yield from gather_hid(k, xall)
        local(xall.at[k], x_out.at[tokens])

        def inputs_by_weights(k, lanes):
            return mm(xall[k], weff[:, lanes], NN)

        yield from scatter_tok(k, inputs_by_weights, ps2, own2, yl2, zs2, zl2, 2 * H)
        gu[k] = own2[k, 1] + zl2[k].astype(F32)
        gate, up = gu[k, :, :H], gu[k, :, H:]
        hall[k, panel, :] = (gate * jax.nn.sigmoid(gate) * up).astype(BF)
        yield from gather_tok(k, hall)
        local(hall.at[k], h_out.at[tokens])

        def hidden_by_down(k, lanes):
            return mm(hall[k], deff[:, lanes], NN)

        yield from scatter_hid(k, hidden_by_down, ss4, sl4, of4, xs4, xl4, zs4, zl4)
        total = scattered(k, of4, zl4)
        eall[k, rows(block, CHIP), mine] = (total - tch[k].astype(F32)).astype(BF)
        osw[k] = total.astype(BF)
        yield from gather_hid(k, eall)
        local(eall.at[k], e_out.at[tokens])

        def error_by_down(k, lanes):
            return mm(eall[k], deff[...], NT)

        yield from scatter_tok(k, error_by_down, ps6, own6, yl6, zs6, zl6, H)
        hidden_grad = own6[k, 1] + zl6[k].astype(F32)
        gate, up = gu[k, :, :H], gu[k, :, H:]
        sigma = jax.nn.sigmoid(gate)
        gall[k, panel, :H] = (hidden_grad * up * (sigma + gate * sigma * (1.0 - sigma))).astype(BF)
        gall[k, panel, H:] = (hidden_grad * (gate * sigma)).astype(BF)
        yield from gather_tok(k, gall)
        local(gall.at[k], g_out.at[tokens])

        def grads_by_weights(k, which):
            return mm(gall[k], weff[which, :], NT)

        yield from scatter_hid(k, grads_by_weights, ss8, sl8, of8, xs8, xl8, zs8, zl8)
        isw[k] = scattered(k, of8, zl8).astype(BF)

    for group in first:
        group.wait_recv()
    for copy in locals_[4:]:
        copy.wait()
    chains = [chain(k) for k in range(CHUNKS)]
    for step in range(STEPS + LAG * (CHUNKS - 1)):
        for k in range(CHUNKS):
            if 0 <= step - k * LAG < STEPS:
                next(chains[k], None)
        if step == 0:
            mask_weights()
    swaps = [send([(held.at[2 * (1 - c) + j], land.at[j], sib) for j in range(2)], land)
             for held, land in ((osw, oland), (isw, iland))]
    for swap, held, land, result in zip(swaps, (osw, isw), (oland, iland), (out, ig)):
        for j in range(2):
            result[pl.ds(j * CHIP, CHIP), mine] = held[2 * c + j]
        swap.wait_recv()
        for j in range(2):
            result[pl.ds(j * CHIP, CHIP), other] = land[j]
    for group in groups:
        group.wait_send()
    for copy in locals_[8:]:
        copy.wait()


def weight_grads(bm, x, h, e, g, out_in, ig_in, out, ig, gwg, uwg, dwg):
    p = pl.program_id(0)
    out[...] = out_in[...]
    ig[...] = ig_in[...]
    value = mm(x[...], g[...], TN)
    for i in range(2):
        for b in range(8):
            to = (gwg, uwg)[b // 4]
            to[pl.ds(i * 128, 128), pl.ds(b % 4 * 128, 128)] = (
                value[i * 128 : i * 128 + 128, b * 128 : b * 128 + 128]
                * (bm[b // 4, b % 4, p * 2 + i].astype(F32) * (1.0 / 32.0))
            )
    value = mm(h[...], e[...], TN)
    for a in range(8):
        dwg[:, pl.ds(a * 128, 128)] = value[:, a * 128 : a * 128 + 128] * (
            bm[2, p, a].astype(F32) * (1.0 / 32.0)
        )


def per_device(student_in, target_delta, gate_weight, up_weight, down_weight, block_mask):
    C = CHUNKS
    block_mask = jnp.swapaxes(block_mask, 1, 2)
    vm = pltpu.VMEM

    def scatter_hid_scratch():
        return [
            vm((C, T, H), F32), vm((C, T, H), F32), vm((C, T, H), F32), vm((C, 3, XB, H), BF), vm((C, 3, XB, H), BF),
            vm((C, 3, CHIP, H), BF), vm((C, 3, CHIP, H), BF), vm((C, CHIP, H), BF), vm((2, CHIP, H), BF),
        ]

    def scatter_tok_scratch(width, far_type):
        return [
            vm((C, T, width), BF), vm((C, 2, Q, width), F32), vm((C, 2, 3, Q, width), BF),
            vm((C, Q, width), far_type), vm((C, Q, width), far_type),
        ]

    vspec = pl.BlockSpec(memory_space=pltpu.VMEM)
    anys = pl.BlockSpec(memory_space=pl.ANY)
    small, square = jax.ShapeDtypeStruct((2 * CHIP, D), BF), jax.ShapeDtypeStruct((C * T, D), BF)
    out, ig, x, h, e, g = pl.pallas_call(
        kernel,
        out_shape=(small, small, square, jax.ShapeDtypeStruct((C * T, H), BF), square, square),
        in_specs=[pl.BlockSpec(memory_space=pltpu.HBM)] * 6,
        out_specs=(vspec, vspec, anys, anys, anys, anys),
        scratch_shapes=[
            vm((D, 2 * H), BF), vm((H, D), BF), vm((C, T, D), BF), vm((C, CHIP, H), BF), vm((T, 2 * H), F32),
            *scatter_tok_scratch(2 * H, F32), vm((C, Q, 2 * H), F32), vm((C, T, H), BF),
            *scatter_hid_scratch(),
            vm((C, T, D), BF), *scatter_tok_scratch(H, BF), vm((C, T, 2 * H), BF),
            *scatter_hid_scratch(),
            vm((D, H), BF), vm((D, H), BF), vm((H, D), BF), pltpu.SMEM((3, 4, 8), jnp.int32),
            pltpu.SemaphoreType.DMA((COPIES,)), pltpu.SemaphoreType.DMA((COPIES,)), pltpu.SemaphoreType.DMA((24,)),
        ],
        compiler_params=pltpu.CompilerParams(
            collective_id=0, has_side_effects=True, vmem_limit_bytes=62 << 20
        ),
        cost_estimate=pl.CostEstimate(flops=6442450944, bytes_accessed=10 << 20, transcendentals=262144),
    )(student_in, target_delta, gate_weight, up_weight, down_weight, block_mask)
    full = lambda *shape: pl.BlockSpec(shape, lambda p: (0, 0))
    return pl.pallas_call(
        weight_grads,
        grid=(4,),
        out_shape=(
            small,
            small,
            jax.ShapeDtypeStruct((D, H), F32),
            jax.ShapeDtypeStruct((D, H), F32),
            jax.ShapeDtypeStruct((H, D), F32),
        ),
        in_specs=[
            pl.BlockSpec(memory_space=pltpu.SMEM),
            pl.BlockSpec((C * T, 256), lambda p: (0, p)),
            pl.BlockSpec((C * T, 128), lambda p: (0, p)),
            full(C * T, D),
            full(C * T, D),
            full(2 * CHIP, D),
            full(2 * CHIP, D),
        ],
        out_specs=(
            full(2 * CHIP, D),
            full(2 * CHIP, D),
            pl.BlockSpec((256, H), lambda p: (p, 0)),
            pl.BlockSpec((256, H), lambda p: (p, 0)),
            pl.BlockSpec((128, D), lambda p: (p, 0)),
        ),
        compiler_params=pltpu.CompilerParams(vmem_limit_bytes=62 << 20),
        cost_estimate=pl.CostEstimate(flops=3221225472, bytes_accessed=13 << 20, transcendentals=0),
    )(block_mask, x, h, e, g, out, ig)


def solution(mesh):
    placed = (
        P("hid", "tok"),
        P("hid", "tok"),
        P("tok", "hid"),
        P("tok", "hid"),
        P("hid", "tok"),
        P(None, "tok", "hid"),
    )
    return jax.shard_map(
        per_device,
        mesh=mesh,
        in_specs=placed,
        out_specs=(
            P("hid", "tok"),
            P("hid", "tok"),
            P("tok", "hid"),
            P("tok", "hid"),
            P("hid", "tok"),
        ),
        check_vma=False,
    )
```

```python
import jax
import jax.numpy as jnp
from jax import lax
from jax.experimental import pallas as pl
from jax.experimental.pallas import tpu as pltpu
from jax.sharding import PartitionSpec as P

BF = jnp.bfloat16
F32 = jnp.float32
CHUNKS = 4
T = 256
CHIP = 16
XB = 4 * CHIP
Q = 32
D = 1024
H = 512
COPIES = 112
STEPS = 23
LAG = 1

NN = (((1,), (0,)), ((), ()))
NT = (((1,), (1,)), ((), ()))
TN = (((0,), (0,)), ((), ()))


def mm(a, b, dims):
    return lax.dot_general(a, b, dims, preferred_element_type=F32)


def kernel(
    x_in, t_in, gw_in, uw_in, dw_in, bm_in,
    out, ig, x_out, h_out, e_out, g_out,
    weff, deff, xall, tch, tmp, ps2, own2, yl2, zs2, zl2, gu, hall,
    ss4, sl4, of4, xs4, xl4, zs4, zl4, osw, oland,
    eall, ps6, own6, yl6, zs6, zl6, gall,
    ss8, sl8, of8, xs8, xl8, zs8, zl8, isw, iland,
    gw, uw, dw, bm,
    send_sems, recv_sems, loc_sems,
):
    tok = lax.axis_index("tok")
    hid = lax.axis_index("hid")
    y, zh = lax.div(tok, 2), lax.rem(tok, 2)
    c, x, zl = lax.rem(hid, 2), lax.rem(lax.div(hid, 2), 4), lax.div(hid, 8)

    def dev(y=y, zh=zh, zl=zl, x=x, c=c):
        return {"tok": y * 2 + zh, "hid": (zl * 4 + x) * 2 + c}

    def plus(a, d):
        return lax.rem(a + d, 4)

    sib = dev(c=1 - c)
    xp = [dev(x=plus(x, d)) for d in (1, 2, 3)]
    zp = [dev(zl=plus(zl, d)) for d in (1, 2, 3)]
    yp = [dev(y=plus(y, d)) for d in (1, 2, 3)]
    far = dev(zh=1 - zh)
    peers = [sib, far] + xp + zp + yp

    def rows(start, size):
        return pl.ds(pl.multiple_of(start, 16), size)

    def half(which):
        return pl.ds(pl.multiple_of(which * H, H), H)

    mine, other = half(c), half(1 - c)
    groups = []

    def send(pairs, whole):
        i = len(groups)
        for src, dst, device in pairs:
            pltpu.make_async_remote_copy(
                src_ref=src, dst_ref=dst, send_sem=send_sems.at[i], recv_sem=recv_sems.at[i],
                device_id=device, device_id_type=pl.DeviceIdType.MESH,
            ).start()
        groups.append(
            pltpu.make_async_remote_copy(
                src_ref=whole, dst_ref=whole, send_sem=send_sems.at[i], recv_sem=recv_sems.at[i],
                device_id=sib, device_id_type=pl.DeviceIdType.MESH,
            )
        )
        return groups[-1]

    locals_ = []

    def local(src, dst):
        copy = pltpu.make_async_copy(src, dst, loc_sems.at[len(locals_)])
        copy.start()
        locals_.append(copy)
        return copy

    barrier = pltpu.get_barrier_semaphore()
    for peer in peers:
        pl.semaphore_signal(barrier, inc=1, device_id=peer, device_id_type=pl.DeviceIdType.MESH)
    for whole, held in ((bm_in, bm), (gw_in, gw), (uw_in, uw), (dw_in, dw)):
        local(whole, held)
    pl.semaphore_wait(barrier, len(peers))

    block = x * XB + zl * CHIP
    first = []
    for whole, buf, at in ((x_in, xall, block), (t_in, tch, 0)):
        for j in range(2):
            src = whole.at[pl.ds(j * CHIP, CHIP)]
            dst = buf.at[2 * c + j, rows(at, CHIP)]
            if whole is x_in:
                first.append(send([(src.at[:, other], dst.at[:, other], sib)], dst.at[:, other]))
                local(src.at[:, mine], dst.at[:, mine])
            else:
                first.append(send([(src.at[:, other], dst, sib)], dst))
                local(src.at[:, mine], dst)

    def mask_weights():
        for copy in locals_[:4]:
            copy.wait()

        @pl.loop(0, 8)
        def _(a):
            at = pl.ds(pl.multiple_of(a * 128, 128), 128)
            for b in range(4):
                lanes = pl.ds(b * 128, 128)
                weff[at, lanes] = (gw[at, lanes].astype(F32) * bm[0, b, a].astype(F32)).astype(BF)
                weff[at, pl.ds(H + b * 128, 128)] = (
                    uw[at, lanes].astype(F32) * bm[1, b, a].astype(F32)
                ).astype(BF)
                deff[lanes, at] = (dw[lanes, at].astype(F32) * bm[2, b, a].astype(F32)).astype(BF)

    def gather_hid(k, buf):
        own = buf.at[k, rows(block, CHIP), mine]
        zc = send([(own, own, p) for p in zp], buf.at[k, pl.ds(0, 3 * CHIP), mine])
        yield
        zc.wait_recv()
        col = buf.at[k, rows(x * XB, XB), mine]
        xc = send([(col, col, xp[d - 1]) for d in (2, 1, 3)], buf.at[k, pl.ds(0, 3 * XB), mine])
        s1 = send([(col, col, sib)], col)
        yield
        xc.wait_recv()
        got = [buf.at[k, rows(plus(x, d) * XB, XB), mine] for d in (1, 2, 3)]
        s2 = send([(g, g, sib) for g in got], buf.at[k, pl.ds(0, 3 * XB), mine])
        yield
        s1.wait_recv()
        s2.wait_recv()

    def scatter_tok(k, product, ps, own, yland, zs, zland, width):
        @pl.loop(0, width // H)
        def _(n):
            lanes = pl.ds(pl.multiple_of(n * H, H), H)
            value = product(k, lanes)
            tmp[:, lanes] = value
            ps[k, :, lanes] = value.astype(BF)

        yc = []
        for part in range(2):
            base = (1 - zh if part == 0 else zh) * 4 * Q
            own[k, part] = tmp[rows(base + y * Q, Q), pl.ds(0, width)]
            yc.append(send([(ps.at[k, rows(base + plus(y, d) * Q, Q)], yland.at[k, part, 3 - d], yp[d - 1])
                            for d in (2, 1, 3)], yland.at[k, part]))
        yield
        yc[0].wait_recv()
        total = own[k, 0]
        for d in range(3):
            total = total + yland[k, 0, d].astype(F32)
        zs[k] = total.astype(zs.dtype)
        zc = send([(zs.at[k], zland.at[k], far)], zland.at[k])
        yield
        yc[1].wait_recv()
        total = own[k, 1]
        for d in range(3):
            total = total + yland[k, 1, d].astype(F32)
        own[k, 1] = total
        yield
        zc.wait_recv()

    def gather_tok(k, buf):
        own = buf.at[k, rows(zh * 4 * Q + y * Q, Q)]
        three = buf.at[k, pl.ds(0, 3 * Q)]
        zc = send([(own, own, far)], own)
        y1 = send([(own, own, yp[d - 1]) for d in (2, 1, 3)], three)
        yield
        zc.wait_recv()
        got = buf.at[k, rows((1 - zh) * 4 * Q + y * Q, Q)]
        y2 = send([(got, got, yp[d - 1]) for d in (2, 1, 3)], three)
        yield
        y1.wait_recv()
        y2.wait_recv()

    def scatter_hid(k, product, ss, sl, of, xs, xl, zs, zland):
        ss[k] = product(k, other).astype(ss.dtype)
        sc = send([(ss.at[k], sl.at[k], sib)], sl.at[k])
        of[k] = product(k, mine)
        yield
        sc.wait_recv()
        pairs = []
        for d in (2, 1, 3):
            at = rows(plus(x, d) * XB, XB)
            xs[k, d - 1] = (of[k, at] + sl[k, at].astype(F32)).astype(BF)
            pairs.append((xs.at[k, d - 1], xl.at[k, 3 - d], xp[d - 1]))
        xc = send(pairs, xl.at[k])
        at = rows(x * XB, XB)
        of[k, at] = of[k, at] + sl[k, at].astype(F32)
        yield
        xc.wait_recv()
        total = of[k, at]
        for d in range(3):
            total = total + xl[k, d].astype(F32)
        of[k, at] = total
        pairs = []
        for d in (1, 2, 3):
            zs[k, d - 1] = of[k, rows(x * XB + plus(zl, d) * CHIP, CHIP)].astype(BF)
            pairs.append((zs.at[k, d - 1], zland.at[k, 3 - d], zp[d - 1]))
        zc = send(pairs, zland.at[k])
        yield
        zc.wait_recv()

    def scattered(k, of, zland):
        total = of[k, rows(block, CHIP)]
        for d in range(3):
            total = total + zland[k, d].astype(F32)
        return total

    def chain(k):
        panel = rows(zh * 4 * Q + y * Q, Q)
        tokens = pl.ds(k * T, T)
        yield from gather_hid(k, xall)
        local(xall.at[k], x_out.at[tokens])

        def inputs_by_weights(k, lanes):
            return mm(xall[k], weff[:, lanes], NN)

        yield from scatter_tok(k, inputs_by_weights, ps2, own2, yl2, zs2, zl2, 2 * H)
        gu[k] = own2[k, 1] + zl2[k].astype(F32)
        gate, up = gu[k, :, :H], gu[k, :, H:]
        hall[k, panel, :] = (gate * jax.nn.sigmoid(gate) * up).astype(BF)
        yield from gather_tok(k, hall)
        local(hall.at[k], h_out.at[tokens])

        def hidden_by_down(k, lanes):
            return mm(hall[k], deff[:, lanes], NN)

        yield from scatter_hid(k, hidden_by_down, ss4, sl4, of4, xs4, xl4, zs4, zl4)
        total = scattered(k, of4, zl4)
        eall[k, rows(block, CHIP), mine] = (total - tch[k].astype(F32)).astype(BF)
        osw[k] = total.astype(BF)
        yield from gather_hid(k, eall)
        local(eall.at[k], e_out.at[tokens])

        def error_by_down(k, lanes):
            return mm(eall[k], deff[...], NT)

        yield from scatter_tok(k, error_by_down, ps6, own6, yl6, zs6, zl6, H)
        hidden_grad = own6[k, 1] + zl6[k].astype(F32)
        gate, up = gu[k, :, :H], gu[k, :, H:]
        sigma = jax.nn.sigmoid(gate)
        gall[k, panel, :H] = (hidden_grad * up * (sigma + gate * sigma * (1.0 - sigma))).astype(BF)
        gall[k, panel, H:] = (hidden_grad * (gate * sigma)).astype(BF)
        yield from gather_tok(k, gall)
        local(gall.at[k], g_out.at[tokens])

        def grads_by_weights(k, which):
            return mm(gall[k], weff[which, :], NT)

        yield from scatter_hid(k, grads_by_weights, ss8, sl8, of8, xs8, xl8, zs8, zl8)
        isw[k] = scattered(k, of8, zl8).astype(BF)

    for group in first:
        group.wait_recv()
    for copy in locals_[4:]:
        copy.wait()
    chains = [chain(k) for k in range(CHUNKS)]
    for step in range(STEPS + LAG * (CHUNKS - 1)):
        for k in range(CHUNKS):
            if 0 <= step - k * LAG < STEPS:
                next(chains[k], None)
        if step == 0:
            mask_weights()
    swaps = [send([(held.at[2 * (1 - c) + j], land.at[j], sib) for j in range(2)], land)
             for held, land in ((osw, oland), (isw, iland))]
    for swap, held, land, result in zip(swaps, (osw, isw), (oland, iland), (out, ig)):
        for j in range(2):
            result[pl.ds(j * CHIP, CHIP), mine] = held[2 * c + j]
        swap.wait_recv()
        for j in range(2):
            result[pl.ds(j * CHIP, CHIP), other] = land[j]
    for group in groups:
        group.wait_send()
    for copy in locals_[8:]:
        copy.wait()


def weight_grads(
    bm_in, x_in, h_in, e_in, g_in, out_in, ig_in,
    out, ig, gwg, uwg, dwg,
    bm, x, h, e, g, gv, uv, dv, in_sems, out_sems,
):
    def start(src, dst, sem):
        copy = pltpu.make_async_copy(src, dst, sem)
        copy.start()
        return copy

    loads = [start(src, dst, in_sems.at[i]) for i, (src, dst) in enumerate(
        ((bm_in, bm), (e_in, e), (h_in, h), (g_in, g), (x_in, x)))]
    stores = [start(out_in, out, out_sems.at[0]), start(ig_in, ig, out_sems.at[1])]

    def store(src, dst):
        stores.append(start(src, dst, out_sems.at[len(stores)]))

    for copy in loads[:3]:
        copy.wait()
    for p in range(2):
        at = pl.ds(p * 256, 256)
        value = mm(h[:, at], e[...], TN)
        for i in range(2):
            for a in range(8):
                dv[pl.ds(p * 256 + i * 128, 128), pl.ds(a * 128, 128)] = value[
                    i * 128 : i * 128 + 128, a * 128 : a * 128 + 128
                ] * (bm[2, p * 2 + i, a].astype(F32) * (1.0 / 32.0))
        store(dv.at[at], dwg.at[at])
    for copy in loads[3:]:
        copy.wait()
    for p in range(4):
        at = pl.ds(p * 256, 256)
        value = mm(x[:, at], g[...], TN)
        for i in range(2):
            for b in range(8):
                to = (gv, uv)[b // 4]
                to[pl.ds(p * 256 + i * 128, 128), pl.ds(b % 4 * 128, 128)] = value[
                    i * 128 : i * 128 + 128, b * 128 : b * 128 + 128
                ] * (bm[b // 4, b % 4, p * 2 + i].astype(F32) * (1.0 / 32.0))
        store(gv.at[at], gwg.at[at])
        store(uv.at[at], uwg.at[at])
    for copy in stores:
        copy.wait()


def per_device(student_in, target_delta, gate_weight, up_weight, down_weight, block_mask):
    C = CHUNKS
    block_mask = jnp.swapaxes(block_mask, 1, 2)
    vm = pltpu.VMEM

    def scatter_hid_scratch():
        return [
            vm((C, T, H), F32), vm((C, T, H), F32), vm((C, T, H), F32), vm((C, 3, XB, H), BF), vm((C, 3, XB, H), BF),
            vm((C, 3, CHIP, H), BF), vm((C, 3, CHIP, H), BF), vm((C, CHIP, H), BF), vm((2, CHIP, H), BF),
        ]

    def scatter_tok_scratch(width, far_type):
        return [
            vm((C, T, width), BF), vm((C, 2, Q, width), F32), vm((C, 2, 3, Q, width), BF),
            vm((C, Q, width), far_type), vm((C, Q, width), far_type),
        ]

    vspec = pl.BlockSpec(memory_space=pltpu.VMEM)
    anys = pl.BlockSpec(memory_space=pl.ANY)
    small, square = jax.ShapeDtypeStruct((2 * CHIP, D), BF), jax.ShapeDtypeStruct((C * T, D), BF)
    out, ig, x, h, e, g = pl.pallas_call(
        kernel,
        out_shape=(small, small, square, jax.ShapeDtypeStruct((C * T, H), BF), square, square),
        in_specs=[pl.BlockSpec(memory_space=pltpu.HBM)] * 6,
        out_specs=(vspec, vspec, anys, anys, anys, anys),
        scratch_shapes=[
            vm((D, 2 * H), BF), vm((H, D), BF), vm((C, T, D), BF), vm((C, CHIP, H), BF), vm((T, 2 * H), F32),
            *scatter_tok_scratch(2 * H, F32), vm((C, Q, 2 * H), F32), vm((C, T, H), BF),
            *scatter_hid_scratch(),
            vm((C, T, D), BF), *scatter_tok_scratch(H, BF), vm((C, T, 2 * H), BF),
            *scatter_hid_scratch(),
            vm((D, H), BF), vm((D, H), BF), vm((H, D), BF), pltpu.SMEM((3, 4, 8), jnp.int32),
            pltpu.SemaphoreType.DMA((COPIES,)), pltpu.SemaphoreType.DMA((COPIES,)), pltpu.SemaphoreType.DMA((24,)),
        ],
        compiler_params=pltpu.CompilerParams(
            collective_id=0, has_side_effects=True, vmem_limit_bytes=62 << 20
        ),
        cost_estimate=pl.CostEstimate(flops=6442450944, bytes_accessed=10 << 20, transcendentals=262144),
    )(student_in, target_delta, gate_weight, up_weight, down_weight, block_mask)
    return pl.pallas_call(
        weight_grads,
        out_shape=(
            small,
            small,
            jax.ShapeDtypeStruct((D, H), F32),
            jax.ShapeDtypeStruct((D, H), F32),
            jax.ShapeDtypeStruct((H, D), F32),
        ),
        in_specs=[anys] * 7,
        out_specs=(anys,) * 5,
        scratch_shapes=[
            pltpu.SMEM((3, 4, 8), jnp.int32), vm((C * T, D), BF), vm((C * T, H), BF), vm((C * T, D), BF),
            vm((C * T, D), BF), vm((D, H), F32), vm((D, H), F32), vm((H, D), F32),
            pltpu.SemaphoreType.DMA((5,)), pltpu.SemaphoreType.DMA((12,)),
        ],
        compiler_params=pltpu.CompilerParams(vmem_limit_bytes=62 << 20),
        cost_estimate=pl.CostEstimate(flops=3221225472, bytes_accessed=13 << 20, transcendentals=0),
    )(block_mask, x, h, e, g, out, ig)


def solution(mesh):
    placed = (
        P("hid", "tok"),
        P("hid", "tok"),
        P("tok", "hid"),
        P("tok", "hid"),
        P("hid", "tok"),
        P(None, "tok", "hid"),
    )
    return jax.shard_map(
        per_device,
        mesh=mesh,
        in_specs=placed,
        out_specs=(
            P("hid", "tok"),
            P("hid", "tok"),
            P("tok", "hid"),
            P("tok", "hid"),
            P("hid", "tok"),
        ),
        check_vma=False,
    )
```

```python
import jax
import jax.numpy as jnp
from jax import lax
from jax.experimental import pallas as pl
from jax.experimental.pallas import tpu as pltpu
from jax.sharding import PartitionSpec as P

BF = jnp.bfloat16
F32 = jnp.float32
CHUNKS = 4
T = 256
CHIP = 16
XB = 4 * CHIP
Q = 32
D = 1024
H = 512
COPIES = 120
STEPS = 23
LAG = 1

NN = (((1,), (0,)), ((), ()))
NT = (((1,), (1,)), ((), ()))
TN = (((0,), (0,)), ((), ()))


def mm(a, b, dims):
    return lax.dot_general(a, b, dims, preferred_element_type=F32)


def kernel(
    x_in, t_in, gw_in, uw_in, dw_in, bm_in,
    out, ig, x_out, h_out, e_out, g_out,
    weff, deff, xall, tch, tmp, ps2, own2, yl2, zs2, zl2, gu, hall,
    ss4, sl4, of4, xs4, xl4, zs4, zl4, osw, oland,
    eall, ps6, own6, yl6, zs6, zl6, gall,
    ss8, sl8, of8, xs8, xl8, zs8, zl8, isw, iland,
    gw, uw, dw, bm,
    send_sems, recv_sems, loc_sems,
):
    tok = lax.axis_index("tok")
    hid = lax.axis_index("hid")
    y, zh = lax.div(tok, 2), lax.rem(tok, 2)
    c, x, zl = lax.rem(hid, 2), lax.rem(lax.div(hid, 2), 4), lax.div(hid, 8)

    def dev(y=y, zh=zh, zl=zl, x=x, c=c):
        return {"tok": y * 2 + zh, "hid": (zl * 4 + x) * 2 + c}

    def plus(a, d):
        return lax.rem(a + d, 4)

    sib = dev(c=1 - c)
    xp = [dev(x=plus(x, d)) for d in (1, 2, 3)]
    zp = [dev(zl=plus(zl, d)) for d in (1, 2, 3)]
    yp = [dev(y=plus(y, d)) for d in (1, 2, 3)]
    far = dev(zh=1 - zh)
    peers = [sib, far] + xp + zp + yp

    def rows(start, size):
        return pl.ds(pl.multiple_of(start, 16), size)

    def half(which):
        return pl.ds(pl.multiple_of(which * H, H), H)

    mine, other = half(c), half(1 - c)
    groups = []

    def send(pairs, whole):
        i = len(groups)
        for src, dst, device in pairs:
            pltpu.make_async_remote_copy(
                src_ref=src, dst_ref=dst, send_sem=send_sems.at[i], recv_sem=recv_sems.at[i],
                device_id=device, device_id_type=pl.DeviceIdType.MESH,
            ).start()
        groups.append(
            pltpu.make_async_remote_copy(
                src_ref=whole, dst_ref=whole, send_sem=send_sems.at[i], recv_sem=recv_sems.at[i],
                device_id=sib, device_id_type=pl.DeviceIdType.MESH,
            )
        )
        return groups[-1]

    locals_ = []

    def local(src, dst):
        copy = pltpu.make_async_copy(src, dst, loc_sems.at[len(locals_)])
        copy.start()
        locals_.append(copy)
        return copy

    barrier = pltpu.get_barrier_semaphore()
    for peer in peers:
        pl.semaphore_signal(barrier, inc=1, device_id=peer, device_id_type=pl.DeviceIdType.MESH)
    for whole, held in ((bm_in, bm), (gw_in, gw), (uw_in, uw), (dw_in, dw)):
        local(whole, held)
    pl.semaphore_wait(barrier, len(peers))

    block = x * XB + zl * CHIP
    first = []
    for whole, buf, at in ((x_in, xall, block), (t_in, tch, 0)):
        for j in range(2):
            src = whole.at[pl.ds(j * CHIP, CHIP)]
            dst = buf.at[2 * c + j, rows(at, CHIP)]
            if whole is x_in:
                first.append(send([(src.at[:, other], dst.at[:, other], sib)], dst.at[:, other]))
                local(src.at[:, mine], dst.at[:, mine])
            else:
                first.append(send([(src.at[:, other], dst, sib)], dst))
                local(src.at[:, mine], dst)

    def mask_weights():
        for copy in locals_[:4]:
            copy.wait()

        @pl.loop(0, 8)
        def _(a):
            at = pl.ds(pl.multiple_of(a * 128, 128), 128)
            for b in range(4):
                lanes = pl.ds(b * 128, 128)
                weff[at, lanes] = (gw[at, lanes].astype(F32) * bm[0, b, a].astype(F32)).astype(BF)
                weff[at, pl.ds(H + b * 128, 128)] = (
                    uw[at, lanes].astype(F32) * bm[1, b, a].astype(F32)
                ).astype(BF)
                deff[lanes, at] = (dw[lanes, at].astype(F32) * bm[2, b, a].astype(F32)).astype(BF)

    def gather_hid(k, buf):
        own = buf.at[k, rows(block, CHIP), mine]
        zc = send([(own, own, p) for p in zp], buf.at[k, pl.ds(0, 3 * CHIP), mine])
        xo = send([(own, own, xp[d - 1]) for d in (2, 1, 3)], buf.at[k, pl.ds(0, 3 * CHIP), mine])
        yield
        zc.wait_recv()
        col = buf.at[k, rows(x * XB, XB), mine]
        rest = [buf.at[k, rows(x * XB + plus(zl, d) * CHIP, CHIP), mine] for d in (1, 2, 3)]
        xc = send([(r, r, xp[d - 1]) for d in (2, 1, 3) for r in rest], buf.at[k, pl.ds(0, 9 * CHIP), mine])
        s1 = send([(col, col, sib)], col)
        yield
        xo.wait_recv()
        xc.wait_recv()
        got = [buf.at[k, rows(plus(x, d) * XB, XB), mine] for d in (1, 2, 3)]
        s2 = send([(g, g, sib) for g in got], buf.at[k, pl.ds(0, 3 * XB), mine])
        yield
        s1.wait_recv()
        s2.wait_recv()

    def scatter_tok(k, product, ps, own, yland, zs, zland, width):
        @pl.loop(0, width // H)
        def _(n):
            lanes = pl.ds(pl.multiple_of(n * H, H), H)
            value = product(k, lanes)
            tmp[:, lanes] = value
            ps[k, :, lanes] = value.astype(BF)

        yc = []
        for part in range(2):
            base = (1 - zh if part == 0 else zh) * 4 * Q
            own[k, part] = tmp[rows(base + y * Q, Q), pl.ds(0, width)]
            yc.append(send([(ps.at[k, rows(base + plus(y, d) * Q, Q)], yland.at[k, part, 3 - d], yp[d - 1])
                            for d in (2, 1, 3)], yland.at[k, part]))
        yield
        yc[0].wait_recv()
        total = own[k, 0]
        for d in range(3):
            total = total + yland[k, 0, d].astype(F32)
        zs[k] = total.astype(zs.dtype)
        zc = send([(zs.at[k], zland.at[k], far)], zland.at[k])
        yield
        yc[1].wait_recv()
        total = own[k, 1]
        for d in range(3):
            total = total + yland[k, 1, d].astype(F32)
        own[k, 1] = total
        yield
        zc.wait_recv()

    def gather_tok(k, buf):
        own = buf.at[k, rows(zh * 4 * Q + y * Q, Q)]
        three = buf.at[k, pl.ds(0, 3 * Q)]
        zc = send([(own, own, far)], own)
        y1 = send([(own, own, yp[d - 1]) for d in (2, 1, 3)], three)
        yield
        zc.wait_recv()
        got = buf.at[k, rows((1 - zh) * 4 * Q + y * Q, Q)]
        y2 = send([(got, got, yp[d - 1]) for d in (2, 1, 3)], three)
        yield
        y1.wait_recv()
        y2.wait_recv()

    def scatter_hid(k, product, ss, sl, of, xs, xl, zs, zland):
        ss[k] = product(k, other).astype(ss.dtype)
        sc = send([(ss.at[k], sl.at[k], sib)], sl.at[k])
        of[k] = product(k, mine)
        yield
        sc.wait_recv()
        pairs = []
        for d in (2, 1, 3):
            at = rows(plus(x, d) * XB, XB)
            xs[k, d - 1] = (of[k, at] + sl[k, at].astype(F32)).astype(BF)
            pairs.append((xs.at[k, d - 1], xl.at[k, 3 - d], xp[d - 1]))
        xc = send(pairs, xl.at[k])
        at = rows(x * XB, XB)
        of[k, at] = of[k, at] + sl[k, at].astype(F32)
        yield
        xc.wait_recv()
        total = of[k, at]
        for d in range(3):
            total = total + xl[k, d].astype(F32)
        of[k, at] = total
        pairs = []
        for d in (1, 2, 3):
            zs[k, d - 1] = of[k, rows(x * XB + plus(zl, d) * CHIP, CHIP)].astype(BF)
            pairs.append((zs.at[k, d - 1], zland.at[k, 3 - d], zp[d - 1]))
        zc = send(pairs, zland.at[k])
        yield
        zc.wait_recv()

    def scattered(k, of, zland):
        total = of[k, rows(block, CHIP)]
        for d in range(3):
            total = total + zland[k, d].astype(F32)
        return total

    def chain(k):
        panel = rows(zh * 4 * Q + y * Q, Q)
        tokens = pl.ds(k * T, T)
        yield from gather_hid(k, xall)
        local(xall.at[k], x_out.at[tokens])

        def inputs_by_weights(k, lanes):
            return mm(xall[k], weff[:, lanes], NN)

        yield from scatter_tok(k, inputs_by_weights, ps2, own2, yl2, zs2, zl2, 2 * H)
        gu[k] = own2[k, 1] + zl2[k].astype(F32)
        gate, up = gu[k, :, :H], gu[k, :, H:]
        hall[k, panel, :] = (gate * jax.nn.sigmoid(gate) * up).astype(BF)
        yield from gather_tok(k, hall)
        local(hall.at[k], h_out.at[tokens])

        def hidden_by_down(k, lanes):
            return mm(hall[k], deff[:, lanes], NN)

        yield from scatter_hid(k, hidden_by_down, ss4, sl4, of4, xs4, xl4, zs4, zl4)
        total = scattered(k, of4, zl4)
        eall[k, rows(block, CHIP), mine] = (total - tch[k].astype(F32)).astype(BF)
        osw[k] = total.astype(BF)
        yield from gather_hid(k, eall)
        local(eall.at[k], e_out.at[tokens])

        def error_by_down(k, lanes):
            return mm(eall[k], deff[...], NT)

        yield from scatter_tok(k, error_by_down, ps6, own6, yl6, zs6, zl6, H)
        hidden_grad = own6[k, 1] + zl6[k].astype(F32)
        gate, up = gu[k, :, :H], gu[k, :, H:]
        sigma = jax.nn.sigmoid(gate)
        gall[k, panel, :H] = (hidden_grad * up * (sigma + gate * sigma * (1.0 - sigma))).astype(BF)
        gall[k, panel, H:] = (hidden_grad * (gate * sigma)).astype(BF)
        yield from gather_tok(k, gall)
        local(gall.at[k], g_out.at[tokens])

        def grads_by_weights(k, which):
            return mm(gall[k], weff[which, :], NT)

        yield from scatter_hid(k, grads_by_weights, ss8, sl8, of8, xs8, xl8, zs8, zl8)
        isw[k] = scattered(k, of8, zl8).astype(BF)

    def swap_own(held, land):
        return send([(held.at[2 * (1 - c) + j], land.at[j], sib) for j in range(2)], land)

    def finish(held, land, result, swap):
        for j in range(2):
            result[pl.ds(j * CHIP, CHIP), mine] = held[2 * c + j]
        swap.wait_recv()
        for j in range(2):
            result[pl.ds(j * CHIP, CHIP), other] = land[j]

    for group in first:
        group.wait_recv()
    for copy in locals_[4:]:
        copy.wait()
    chains = [chain(k) for k in range(CHUNKS)]
    for step in range(STEPS + LAG * (CHUNKS - 1)):
        for k in range(CHUNKS):
            if 0 <= step - k * LAG < STEPS:
                next(chains[k], None)
        if step == 0:
            mask_weights()
        if step == 16:
            out_swap = swap_own(osw, oland)
        if step == 18:
            finish(osw, oland, out, out_swap)
    finish(isw, iland, ig, swap_own(isw, iland))
    for group in groups:
        group.wait_send()
    for copy in locals_[8:]:
        copy.wait()


def weight_grads(
    bm_in, x_in, h_in, e_in, g_in, out_in, ig_in,
    out, ig, gwg, uwg, dwg,
    bm, x, h, e, g, gv, uv, dv, in_sems, out_sems,
):
    def start(src, dst, sem):
        copy = pltpu.make_async_copy(src, dst, sem)
        copy.start()
        return copy

    loads = [start(src, dst, in_sems.at[i]) for i, (src, dst) in enumerate(
        ((bm_in, bm), (e_in, e), (h_in, h), (g_in, g), (x_in, x)))]
    stores = [start(out_in, out, out_sems.at[0]), start(ig_in, ig, out_sems.at[1])]

    def store(src, dst):
        stores.append(start(src, dst, out_sems.at[len(stores)]))

    for copy in loads[:3]:
        copy.wait()
    for p in range(2):
        at = pl.ds(p * 256, 256)
        value = mm(h[:, at], e[...], TN)
        for i in range(2):
            for a in range(8):
                dv[pl.ds(p * 256 + i * 128, 128), pl.ds(a * 128, 128)] = value[
                    i * 128 : i * 128 + 128, a * 128 : a * 128 + 128
                ] * (bm[2, p * 2 + i, a].astype(F32) * (1.0 / 32.0))
        store(dv.at[at], dwg.at[at])
    for copy in loads[3:]:
        copy.wait()
    for p in range(4):
        at = pl.ds(p * 256, 256)
        value = mm(x[:, at], g[...], TN)
        for i in range(2):
            for b in range(8):
                to = (gv, uv)[b // 4]
                to[pl.ds(p * 256 + i * 128, 128), pl.ds(b % 4 * 128, 128)] = value[
                    i * 128 : i * 128 + 128, b * 128 : b * 128 + 128
                ] * (bm[b // 4, b % 4, p * 2 + i].astype(F32) * (1.0 / 32.0))
        store(gv.at[at], gwg.at[at])
        store(uv.at[at], uwg.at[at])
    for copy in stores:
        copy.wait()


def per_device(student_in, target_delta, gate_weight, up_weight, down_weight, block_mask):
    C = CHUNKS
    block_mask = jnp.swapaxes(block_mask, 1, 2)
    vm = pltpu.VMEM

    def scatter_hid_scratch():
        return [
            vm((C, T, H), F32), vm((C, T, H), F32), vm((C, T, H), F32), vm((C, 3, XB, H), BF), vm((C, 3, XB, H), BF),
            vm((C, 3, CHIP, H), BF), vm((C, 3, CHIP, H), BF), vm((C, CHIP, H), BF), vm((2, CHIP, H), BF),
        ]

    def scatter_tok_scratch(width, far_type):
        return [
            vm((C, T, width), BF), vm((C, 2, Q, width), F32), vm((C, 2, 3, Q, width), BF),
            vm((C, Q, width), far_type), vm((C, Q, width), far_type),
        ]

    vspec = pl.BlockSpec(memory_space=pltpu.VMEM)
    anys = pl.BlockSpec(memory_space=pl.ANY)
    small, square = jax.ShapeDtypeStruct((2 * CHIP, D), BF), jax.ShapeDtypeStruct((C * T, D), BF)
    out, ig, x, h, e, g = pl.pallas_call(
        kernel,
        out_shape=(small, small, square, jax.ShapeDtypeStruct((C * T, H), BF), square, square),
        in_specs=[pl.BlockSpec(memory_space=pltpu.HBM)] * 6,
        out_specs=(vspec, vspec, anys, anys, anys, anys),
        scratch_shapes=[
            vm((D, 2 * H), BF), vm((H, D), BF), vm((C, T, D), BF), vm((C, CHIP, H), BF), vm((T, 2 * H), F32),
            *scatter_tok_scratch(2 * H, F32), vm((C, Q, 2 * H), F32), vm((C, T, H), BF),
            *scatter_hid_scratch(),
            vm((C, T, D), BF), *scatter_tok_scratch(H, BF), vm((C, T, 2 * H), BF),
            *scatter_hid_scratch(),
            vm((D, H), BF), vm((D, H), BF), vm((H, D), BF), pltpu.SMEM((3, 4, 8), jnp.int32),
            pltpu.SemaphoreType.DMA((COPIES,)), pltpu.SemaphoreType.DMA((COPIES,)), pltpu.SemaphoreType.DMA((24,)),
        ],
        compiler_params=pltpu.CompilerParams(
            collective_id=0, has_side_effects=True, vmem_limit_bytes=62 << 20
        ),
        cost_estimate=pl.CostEstimate(flops=6442450944, bytes_accessed=10 << 20, transcendentals=262144),
    )(student_in, target_delta, gate_weight, up_weight, down_weight, block_mask)
    return pl.pallas_call(
        weight_grads,
        out_shape=(
            small,
            small,
            jax.ShapeDtypeStruct((D, H), F32),
            jax.ShapeDtypeStruct((D, H), F32),
            jax.ShapeDtypeStruct((H, D), F32),
        ),
        in_specs=[anys] * 7,
        out_specs=(anys,) * 5,
        scratch_shapes=[
            pltpu.SMEM((3, 4, 8), jnp.int32), vm((C * T, D), BF), vm((C * T, H), BF), vm((C * T, D), BF),
            vm((C * T, D), BF), vm((D, H), F32), vm((D, H), F32), vm((H, D), F32),
            pltpu.SemaphoreType.DMA((5,)), pltpu.SemaphoreType.DMA((12,)),
        ],
        compiler_params=pltpu.CompilerParams(vmem_limit_bytes=62 << 20),
        cost_estimate=pl.CostEstimate(flops=3221225472, bytes_accessed=13 << 20, transcendentals=0),
    )(block_mask, x, h, e, g, out, ig)


def solution(mesh):
    placed = (
        P("hid", "tok"),
        P("hid", "tok"),
        P("tok", "hid"),
        P("tok", "hid"),
        P("hid", "tok"),
        P(None, "tok", "hid"),
    )
    return jax.shard_map(
        per_device,
        mesh=mesh,
        in_specs=placed,
        out_specs=(
            P("hid", "tok"),
            P("hid", "tok"),
            P("tok", "hid"),
            P("tok", "hid"),
            P("hid", "tok"),
        ),
        check_vma=False,
    )
```
